32 devices in a mesh: row: 16 (over z, y, core), col: 2 (over x).
Axes of the slice: x: 2, y: 2, z: 4, core: 2. Of those that a mesh axis runs over, the one named last changes fastest.
Arguments:
- currents: float32 [8, 131072], P(None, ('row', 'col')), may hold values from -6 to 6
- src_pos: float32 [3, 131072], P(None, ('row', 'col')), may hold values from 0 to 1
- src_dir: float32 [3, 131072], P(None, ('row', 'col')), may hold values from -1 to 1
- cell_ends: int32 [2, 131072], P(None, ('row', 'col')), may hold values from 0 to 65535, as said below
- pan_pos: float32 [3, 65536], P(None, ('row', 'col')), may hold values from 0 to 1
- tgt_pos: float32 [3, 4096], P(None, 'row'), may hold values from 0 to 1
- tgt_dir: float32 [3, 4096], P(None, 'row'), may hold values from -1 to 1
- tgt_ends: int32 [2, 4096], P(None, 'row'), may hold values from 0 to 2047, as said below
- wpan_pos: float32 [3, 2048], P(None, 'row'), may hold values from 0 to 1
Outputs:
- voltage: float32 [8, 4096], P(None, ('row', 'col'))
The draws below stay inside these ranges and needn't reach their ends.
Inputs may be any that keep to these rules, and one draw needn't show every extreme that they name: `cell_ends`: A cell's two panels differ. Source cell j and its panels belong to devices with the same col index: with b = j // 4096 and c = p // 2048, b and c leave the same remainder on division by 2. `tgt_ends`: A target cell's two panels differ.
All inputs are finite; a program needn't handle non-finite values.
Results may differ from the reference program's by a relative error of at most 0.006.
Values may be sent and summed in bfloat16 or wider, within the bound.
A program may use at most 192 MiB of HBM per device.

```python
import math
import jax
import jax.numpy as jnp
from jax import lax

CELLS = 131072
PANELS = 65536
PORTS = 4
ROWS = 4096
PROWS = 2048
CELL_DEV = 4096
PANEL_DEV = 2048
PANEL_BLOCK = 32768


def draw_cell_ends(key, part):
    first_key, step_key = jax.random.split(jax.random.fold_in(key, 11))
    first = jax.random.randint(first_key, (CELLS,), 0, PANEL_BLOCK)
    first = first.at[0].set(0).at[CELLS - 1].set(PANEL_BLOCK - 1)
    offset = jax.random.randint(step_key, (CELLS,), 1, PANEL_BLOCK)
    second = (first + offset) % PANEL_BLOCK
    groups = PANELS // PANEL_BLOCK
    column = jnp.arange(CELLS, dtype=jnp.int32) // CELL_DEV % groups

    def to_global(local):
        return (local // PANEL_DEV * groups + column) * PANEL_DEV + local % PANEL_DEV
    return jnp.stack([to_global(first), to_global(second)]).astype(jnp.int32)


def draw_tgt_ends(key, part):
    first_key, step_key = jax.random.split(jax.random.fold_in(key, 23))
    first = jax.random.randint(first_key, (ROWS,), 0, PROWS)
    first = first.at[0].set(0).at[ROWS - 1].set(PROWS - 1)
    offset = jax.random.randint(step_key, (ROWS,), 1, PROWS)
    second = (first + offset) % PROWS
    return jnp.stack([first, second]).astype(jnp.int32)


def block_scale(own_key, extent, cuts, least, top_value):
    def one(dim, shards_of):
        heights = jax.random.uniform(jax.random.fold_in(jax.random.fold_in(own_key, 6), dim), (shards_of,), jnp.float32, least / len(cuts), top_value / len(cuts))
        return jnp.repeat(jnp.exp(heights), extent[dim] // shards_of).reshape((-1,) + (1,) * (len(extent) - dim - 1))

    level = one(*cuts[0])
    for cut in cuts[1:]:
        level = level * one(*cut)
    return level


def noise(own_key, shape, scale, reach, cuts=(), kind=jnp.bfloat16):
    level = block_scale(own_key, shape, cuts, -0.22, 0.18) if cuts else 1.0
    values = jax.random.normal(own_key, shape, jnp.float32) * scale * level
    return jnp.minimum(jnp.maximum(values, -reach), reach).astype(kind)


def setup_inputs(seed: int = 0) -> dict:
    key_of = jax.random.split(jax.random.key(seed), 10)
    currents = noise(key_of[0], (2 * PORTS, CELLS), 1.0, 6.0, ((1, 32),), jnp.float32)
    src_pos = jnp.clip(1.0 * jax.random.uniform(key_of[1], (3, CELLS), jnp.float32) ** block_scale(key_of[1], (3, CELLS), ((1, 32),), -0.2, 0.2), 0.0, 1.0)
    src_dir = jnp.clip(jax.random.uniform(key_of[2], (3, CELLS), jnp.float32, -1.0, 1.0) * block_scale(key_of[2], (3, CELLS), ((1, 32),), -0.4, 0.0), -1.0, 1.0)
    cell_ends = draw_cell_ends(jax.random.fold_in(key_of[9], 71), 0)
    pan_pos = jnp.clip(1.0 * jax.random.uniform(key_of[4], (3, PANELS), jnp.float32) ** block_scale(key_of[4], (3, PANELS), ((1, 32),), -0.2, 0.2), 0.0, 1.0)
    tgt_pos = jnp.clip(1.0 * jax.random.uniform(key_of[5], (3, ROWS), jnp.float32) ** block_scale(key_of[5], (3, ROWS), ((1, 16),), -0.2, 0.2), 0.0, 1.0)
    tgt_dir = jnp.clip(jax.random.uniform(key_of[6], (3, ROWS), jnp.float32, -1.0, 1.0) * block_scale(key_of[6], (3, ROWS), ((1, 16),), -0.4, 0.0), -1.0, 1.0)
    tgt_ends = draw_tgt_ends(jax.random.fold_in(key_of[9], 71), 0)
    wpan_pos = jnp.clip(1.0 * jax.random.uniform(key_of[8], (3, PROWS), jnp.float32) ** block_scale(key_of[8], (3, PROWS), ((1, 16),), -0.2, 0.2), 0.0, 1.0)
    return dict(currents=currents, src_pos=src_pos, src_dir=src_dir, cell_ends=cell_ends, pan_pos=pan_pos, tgt_pos=tgt_pos, tgt_dir=tgt_dir, tgt_ends=tgt_ends, wpan_pos=wpan_pos)


soft_sq = 0.0004
wave_num = 12.0

def kernel_tile(tpos, spos, tdir, sdir):
    dx = tpos[0][:, None] - spos[0][None, :]
    dy = tpos[1][:, None] - spos[1][None, :]
    dz = tpos[2][:, None] - spos[2][None, :]
    dist_sq = dx * dx + dy * dy + dz * dz + soft_sq
    inverse = lax.rsqrt(dist_sq)
    phase = wave_num * dist_sq * inverse
    real_part = jnp.cos(phase) * inverse
    imag_part = -jnp.sin(phase) * inverse
    if tdir is not None:
        inner = tdir[0][:, None] * sdir[0][None, :] + tdir[1][:, None] * sdir[1][None, :] + tdir[2][:, None] * sdir[2][None, :]
        real_part = real_part * inner
        imag_part = imag_part * inner
    return jnp.concatenate([real_part, imag_part], axis=1).astype(jnp.bfloat16)

def apply_tile(stacked, source):
    half = source.shape[0] // 2
    real_src = source[:half]
    imag_src = source[half:]
    left = jnp.concatenate([jnp.concatenate([real_src, -imag_src], 1), jnp.concatenate([imag_src, real_src], 1)], 0)
    return lax.dot_general(left, stacked, (((1,), (1,)), ((), ())), preferred_element_type=jnp.float32)

def reference(currents, src_pos, src_dir, cell_ends, pan_pos, tgt_pos, tgt_dir, tgt_ends, wpan_pos):
    cur16 = currents.astype(jnp.bfloat16)
    width = min(2048, CELLS)
    count = CELLS // width

    def cell_step(total, index):
        start = (index * width).astype(jnp.int32)
        spos = lax.dynamic_slice_in_dim(src_pos, start, width, 1)
        sdir = lax.dynamic_slice_in_dim(src_dir, start, width, 1)
        source = lax.dynamic_slice_in_dim(cur16, start, width, 1)
        return (total + apply_tile(kernel_tile(tgt_pos, spos, tgt_dir, sdir), source), None)
    induct, _ = lax.scan(cell_step, jnp.zeros((2 * PORTS, ROWS), jnp.float32), jnp.arange(count, dtype=jnp.int32))
    cur_wide = cur16.astype(jnp.float32)
    charges = jnp.zeros((2 * PORTS, PANELS), jnp.float32)
    charges = charges.at[:, cell_ends[0]].add(cur_wide).at[:, cell_ends[1]].add(-cur_wide)
    q16 = charges.astype(jnp.bfloat16)
    pwidth = min(2048, PANELS)
    pcount = PANELS // pwidth

    def panel_step(total, index):
        start = (index * pwidth).astype(jnp.int32)
        ppos = lax.dynamic_slice_in_dim(pan_pos, start, pwidth, 1)
        source = lax.dynamic_slice_in_dim(q16, start, pwidth, 1)
        return (total + apply_tile(kernel_tile(wpan_pos, ppos, None, None), source), None)
    field, _ = lax.scan(panel_step, jnp.zeros((2 * PORTS, PROWS), jnp.float32), jnp.arange(pcount, dtype=jnp.int32))
    pscale = 0.25 / math.sqrt(PANELS)
    lscale = 1.0 / math.sqrt(CELLS)
    potential = jnp.concatenate([field[PORTS:], -field[:PORTS]], 0) * pscale
    voltage = jnp.concatenate([-induct[PORTS:], induct[:PORTS]], 0) * lscale
    return voltage + jnp.take(potential, tgt_ends[0], axis=1) - jnp.take(potential, tgt_ends[1], axis=1)
```

```python
import functools
import math

import jax
import jax.numpy as jnp
from jax import lax
from jax.experimental import pallas as pl
from jax.experimental.pallas import tpu as pltpu
from jax.sharding import PartitionSpec as P

CELLS = 131072
PANELS = 65536

soft_sq = 0.0004
wave_num = 12.0
turn = wave_num / (2 * math.pi)

A1, A0, K1 = -2.24750753, 1.37545559, 2.2830122
B2, B1, B0 = -3.52005613, 4.32182737, -0.87613445
ENTRY = 2 * K1 * K1
MAGIC = 12582912.0

F32 = jnp.float32
BF16 = jnp.bfloat16


def split3(x):
    a = lax.reduce_precision(x, 8, 7)
    b = lax.reduce_precision(x - a, 8, 7)
    c = lax.reduce_precision(x - a - b, 8, 7)
    return a, b, c


def point_features(pos, is_target):
    x = (pos - 0.5) * turn
    sq = jnp.sum(x * x, axis=0, keepdims=True)
    if is_target:
        sq = sq + soft_sq * turn * turn
        x = -2.0 * x
    a, b, c = split3(x)
    n = split3(sq)
    one = jnp.ones((3, pos.shape[1]), F32)
    pad = jnp.zeros((8, pos.shape[1]), F32)
    if is_target:
        rows = [a, a, a, b, b, c, *n, one, pad]
    else:
        rows = [a, b, c, a, b, a, one, *n, pad]
    return jnp.concatenate(rows, 0).astype(BF16)


def vector_features(vec, is_target):
    a, b, c = split3(vec)
    pad = jnp.zeros((14, vec.shape[1]), F32)
    rows = [a, a, a, b, b, c, pad] if is_target else [a, b, c, a, b, a, pad]
    return jnp.concatenate(rows, 0).astype(BF16)


def entries(dist, weight):
    inverse = lax.rsqrt(dist)
    phase = dist * inverse
    f = phase - ((phase + MAGIC) - MAGIC)
    z = f * f
    s = ((z + A1) * z + A0) * f
    c = ((z + B2) * z + B1) * z + B0
    m = inverse if weight is None else inverse * weight
    real_part = (1.0 / ENTRY - s * s) * m
    imag_part = (s * m) * c
    return real_part.astype(BF16), imag_part.astype(BF16)


def dot(a, b, da, db):
    return lax.dot_general(a, b, (((da,), (db,)), ((), ())), preferred_element_type=F32)


def sweep_kernel(tb, sb, unroll, with_dir, *refs):
    if with_dir:
        ft, fs, gt, gs, wr, wi, out = refs
    else:
        ft, fs, wr, wi, out = refs
    targets = ft.shape[1]
    sources = fs.shape[0]

    @pl.loop(0, targets // tb)
    def _(t):
        tcol = pl.ds(pl.multiple_of(t * tb, tb), tb)
        fcol = ft[:, tcol]
        gcol = gt[:, tcol] if with_dir else None

        def step(j, acc):
            for u in range(unroll):
                start = pl.multiple_of((j * unroll + u) * sb, sb)
                rows = pl.ds(start, sb)
                dist = dot(fs[rows, :], fcol, 1, 0)
                weight = dot(gs[rows, :], gcol, 1, 0) if with_dir else None
                re, im = entries(dist, weight)
                acc = acc + dot(wr[:, rows], re, 1, 0) + dot(wi[:, rows], im, 1, 0)
            return acc

        out[:, tcol] = lax.fori_loop(
            0, sources // (sb * unroll), step, jnp.zeros((wr.shape[0], tb), F32)
        )


def sweep(ft, fs, gt, gs, source, tb=256, sb=256, unroll=2):
    half = source.shape[0] // 2
    targets, sources = ft.shape[1], fs.shape[0]
    tb, sb = min(tb, targets), min(sb, sources)
    unroll = min(unroll, sources // sb)
    wi = jnp.concatenate([-0.5 * source[half:], 0.5 * source[:half]], 0)
    args = (ft, fs, source, wi) if gt is None else (ft, fs, gt, gs, source, wi)
    total = targets * sources
    out = pl.pallas_call(
        functools.partial(sweep_kernel, tb, sb, unroll, gt is not None),
        out_shape=jax.ShapeDtypeStruct((source.shape[0], targets), F32),
        in_specs=[pl.BlockSpec(memory_space=pltpu.VMEM)] * len(args),
        out_specs=pl.BlockSpec(memory_space=pltpu.VMEM),
        compiler_params=pltpu.CompilerParams(vmem_limit_bytes=40 * 2**20),
        cost_estimate=pl.CostEstimate(
            flops=total * 1600, bytes_accessed=4 * 2**20, transcendentals=total
        ),
        name="sweep_cells" if gt is not None else "sweep_panels",
    )(*args)
    return out * (ENTRY * turn)


def spread_kernel(ends, cur, out):
    doubled = cur.shape[0]
    lows = out.shape[1]
    highs = out.shape[0] // doubled
    n = ends.shape[1]
    chunk = min(n, 512)

    def step(j, acc):
        cols = pl.ds(pl.multiple_of(j * chunk, chunk), chunk)
        for e in range(2):
            idx = ends[e : e + 1, cols]
            hi = idx // lows
            lo = idx - hi * lows
            hit = lax.broadcasted_iota(jnp.int32, (highs, chunk), 0) == hi
            low = jnp.where(
                lax.broadcasted_iota(jnp.int32, (lows, chunk), 0) == lo, 1.0 - 2.0 * e, 0.0
            ).astype(BF16)
            rows = [jnp.where(hit, cur[r : r + 1, cols], 0.0) for r in range(doubled)]
            acc = acc + dot(jnp.concatenate(rows, 0).astype(BF16), low, 1, 1)
        return acc

    out[...] = lax.fori_loop(0, n // chunk, step, jnp.zeros(out.shape, F32))


def spread(ends, cur_wide, block_len):
    doubled = cur_wide.shape[0]
    lows = 256
    highs = block_len // lows
    out = pl.pallas_call(
        spread_kernel,
        out_shape=jax.ShapeDtypeStruct((doubled * highs, lows), F32),
        in_specs=[pl.BlockSpec(memory_space=pltpu.VMEM)] * 2,
        out_specs=pl.BlockSpec(memory_space=pltpu.VMEM),
        compiler_params=pltpu.CompilerParams(vmem_limit_bytes=40 * 2**20),
        name="spread_charges",
    )(ends, cur_wide)
    return out.reshape(doubled, block_len)


def ends_kernel(ends, pot, base, out):
    tb = 256
    panels = pot.shape[1]
    a, b, c = split3(pot[...])
    a, b, c = a.astype(BF16), b.astype(BF16), c.astype(BF16)
    pieces = jnp.concatenate([a, b, c, jnp.zeros_like(a)], 0)
    d = a.shape[0]

    @pl.loop(0, ends.shape[1] // tb)
    def _(t):
        cols = pl.ds(pl.multiple_of(t * tb, tb), tb)
        row = lax.broadcasted_iota(jnp.int32, (panels, tb), 0)
        pick = jnp.where(row == ends[0:1, cols], 1.0, 0.0) - jnp.where(
            row == ends[1:2, cols], 1.0, 0.0
        )
        got = dot(pieces, pick.astype(BF16), 1, 0)
        out[:, cols] = base[:, cols] + (got[:d] + got[d : 2 * d]) + got[2 * d : 3 * d]


def end_difference(ends, pot, base):
    return pl.pallas_call(
        ends_kernel,
        out_shape=jax.ShapeDtypeStruct(base.shape, F32),
        in_specs=[pl.BlockSpec(memory_space=pltpu.VMEM)] * 3,
        out_specs=pl.BlockSpec(memory_space=pltpu.VMEM),
        compiler_params=pltpu.CompilerParams(vmem_limit_bytes=40 * 2**20),
        name="end_difference",
    )(ends, pot, base)


def per_device(
    currents, src_pos, src_dir, cell_ends, pan_pos, tgt_pos, tgt_dir, tgt_ends, wpan_pos
):
    doubled = currents.shape[0]
    half = doubled // 2
    col_count = lax.axis_size("col")
    rows = lax.axis_size("row")
    panel_dev = pan_pos.shape[1]
    block_len = panel_dev * rows
    tdev, wdev = tgt_pos.shape[1], wpan_pos.shape[1]
    packed = jnp.concatenate(
        [tgt_pos.reshape(-1), tgt_dir.reshape(-1), wpan_pos.reshape(-1)]
    ).reshape(1, -1, 128)
    packed = lax.all_gather(packed, "row", axis=0, tiled=True).reshape(rows, -1)
    tend = lax.all_gather(tgt_ends, "row", axis=1, tiled=True)

    cur16 = currents.astype(BF16)
    cur_wide = lax.reduce_precision(currents, 8, 7)
    local_ends = cell_ends // (panel_dev * col_count) * panel_dev + cell_ends % panel_dev
    partial_value = spread(local_ends, cur_wide, block_len)
    charge = lax.psum_scatter(partial_value, "row", scatter_dimension=1, tiled=True)

    def whole(start, width):
        piece = packed[:, start : start + 3 * width].reshape(rows, 3, width)
        return piece.transpose(1, 0, 2).reshape(3, rows * width)

    tpos = whole(0, tdev)
    tdir = whole(3 * tdev, tdev)
    wpos = whole(6 * tdev, wdev)
    induct = sweep(
        point_features(tpos, True),
        point_features(src_pos, False).T,
        vector_features(tdir, True),
        vector_features(src_dir, False).T,
        cur16,
    )
    field = sweep(
        point_features(wpos, True),
        point_features(pan_pos, False).T,
        None,
        None,
        charge.astype(BF16),
    )
    pscale = 0.25 / math.sqrt(PANELS)
    lscale = 1.0 / math.sqrt(CELLS)
    potential = jnp.concatenate([field[half:], -field[:half]], 0) * pscale
    voltage = jnp.concatenate([-induct[half:], induct[:half]], 0) * lscale
    total = end_difference(tend, potential, voltage)
    return lax.psum_scatter(total, ("row", "col"), scatter_dimension=1, tiled=True)


def solution(mesh):
    return jax.shard_map(
        per_device,
        mesh=mesh,
        in_specs=(
            P(None, ("row", "col")),
            P(None, ("row", "col")),
            P(None, ("row", "col")),
            P(None, ("row", "col")),
            P(None, ("row", "col")),
            P(None, "row"),
            P(None, "row"),
            P(None, "row"),
            P(None, "row"),
        ),
        out_specs=P(None, ("row", "col")),
        check_vma=False,
    )
```

```python
import functools
import math

import jax
import jax.numpy as jnp
from jax import lax
from jax.experimental import pallas as pl
from jax.experimental.pallas import tpu as pltpu
from jax.sharding import PartitionSpec as P

CELLS = 131072
PANELS = 65536

soft_sq = 0.0004
wave_num = 12.0
turn = wave_num / (2 * math.pi)

A1, A0, K1 = -2.24750753, 1.37545559, 2.2830122
B2, B1, B0 = -3.52005613, 4.32182737, -0.87613445
ENTRY = 2 * K1 * K1
MAGIC = 12582912.0

F32 = jnp.float32
BF16 = jnp.bfloat16


def split3(x):
    a = lax.reduce_precision(x, 8, 7)
    b = lax.reduce_precision(x - a, 8, 7)
    c = lax.reduce_precision(x - a - b, 8, 7)
    return a, b, c


def point_features(pos, is_target):
    x = (pos - 0.5) * turn
    sq = jnp.sum(x * x, axis=0, keepdims=True)
    if is_target:
        sq = sq + soft_sq * turn * turn
        x = -2.0 * x
    a, b, c = split3(x)
    n = split3(sq)
    one = jnp.ones((3, pos.shape[1]), F32)
    pad = jnp.zeros((8, pos.shape[1]), F32)
    if is_target:
        rows = [a, a, a, b, b, c, *n, one, pad]
    else:
        rows = [a, b, c, a, b, a, one, *n, pad]
    return jnp.concatenate(rows, 0).astype(BF16)


def vector_features(vec, is_target):
    a, b, c = split3(vec)
    pad = jnp.zeros((14, vec.shape[1]), F32)
    rows = [a, a, a, b, b, c, pad] if is_target else [a, b, c, a, b, a, pad]
    return jnp.concatenate(rows, 0).astype(BF16)


def entries(dist, weight):
    inverse = lax.rsqrt(dist)
    phase = dist * inverse
    f = phase - ((phase + MAGIC) - MAGIC)
    z = f * f
    s = ((z + A1) * z + A0) * f
    c = ((z + B2) * z + B1) * z + B0
    m = inverse if weight is None else inverse * weight
    real_part = (1.0 / ENTRY - s * s) * m
    imag_part = (s * m) * c
    return real_part.astype(BF16), imag_part.astype(BF16)


def dot(a, b, da, db):
    return lax.dot_general(a, b, (((da,), (db,)), ((), ())), preferred_element_type=F32)


def sweep_kernel(tb, sb, unroll, with_dir, *refs):
    if with_dir:
        ft, fs, gt, gs, wr, wi, out = refs
    else:
        ft, fs, wr, wi, out = refs
    targets = ft.shape[1]
    sources = fs.shape[0]

    @pl.loop(0, targets // tb)
    def _(t):
        tcol = pl.ds(pl.multiple_of(t * tb, tb), tb)
        fcol = ft[:, tcol]
        gcol = gt[:, tcol] if with_dir else None

        def step(j, acc):
            for u in range(unroll):
                start = pl.multiple_of((j * unroll + u) * sb, sb)
                rows = pl.ds(start, sb)
                dist = dot(fs[rows, :], fcol, 1, 0)
                weight = dot(gs[rows, :], gcol, 1, 0) if with_dir else None
                re, im = entries(dist, weight)
                acc = acc + dot(wr[:, rows], re, 1, 0) + dot(wi[:, rows], im, 1, 0)
            return acc

        out[:, tcol] = lax.fori_loop(
            0, sources // (sb * unroll), step, jnp.zeros((wr.shape[0], tb), F32)
        )


def sweep(ft, fs, gt, gs, source, tb=1024, sb=128, unroll=2):
    half = source.shape[0] // 2
    targets, sources = ft.shape[1], fs.shape[0]
    tb, sb = min(tb, targets), min(sb, sources)
    unroll = min(unroll, sources // sb)
    wi = jnp.concatenate([-0.5 * source[half:], 0.5 * source[:half]], 0)
    args = (ft, fs, source, wi) if gt is None else (ft, fs, gt, gs, source, wi)
    total = targets * sources
    out = pl.pallas_call(
        functools.partial(sweep_kernel, tb, sb, unroll, gt is not None),
        out_shape=jax.ShapeDtypeStruct((source.shape[0], targets), F32),
        in_specs=[pl.BlockSpec(memory_space=pltpu.VMEM)] * len(args),
        out_specs=pl.BlockSpec(memory_space=pltpu.VMEM),
        compiler_params=pltpu.CompilerParams(vmem_limit_bytes=40 * 2**20),
        cost_estimate=pl.CostEstimate(
            flops=total * 1600, bytes_accessed=4 * 2**20, transcendentals=total
        ),
        name="sweep_cells" if gt is not None else "sweep_panels",
    )(*args)
    return out * (ENTRY * turn)


def spread_kernel(ends, cur, out):
    doubled = cur.shape[0]
    lows = out.shape[1]
    highs = out.shape[0] // doubled
    n = ends.shape[1]
    chunk = min(n, 512)

    def step(j, acc):
        cols = pl.ds(pl.multiple_of(j * chunk, chunk), chunk)
        for e in range(2):
            idx = ends[e : e + 1, cols]
            hi = idx // lows
            lo = idx - hi * lows
            hit = lax.broadcasted_iota(jnp.int32, (highs, chunk), 0) == hi
            low = jnp.where(
                lax.broadcasted_iota(jnp.int32, (lows, chunk), 0) == lo, 1.0 - 2.0 * e, 0.0
            ).astype(BF16)
            rows = [jnp.where(hit, cur[r : r + 1, cols], 0.0) for r in range(doubled)]
            acc = acc + dot(jnp.concatenate(rows, 0).astype(BF16), low, 1, 1)
        return acc

    out[...] = lax.fori_loop(0, n // chunk, step, jnp.zeros(out.shape, F32))


def spread(ends, cur_wide, block_len):
    doubled = cur_wide.shape[0]
    lows = 256
    highs = block_len // lows
    out = pl.pallas_call(
        spread_kernel,
        out_shape=jax.ShapeDtypeStruct((doubled * highs, lows), F32),
        in_specs=[pl.BlockSpec(memory_space=pltpu.VMEM)] * 2,
        out_specs=pl.BlockSpec(memory_space=pltpu.VMEM),
        compiler_params=pltpu.CompilerParams(vmem_limit_bytes=40 * 2**20),
        name="spread_charges",
    )(ends, cur_wide)
    return out.reshape(doubled, block_len)


def ends_kernel(ends, pot, base, out):
    tb = 256
    panels = pot.shape[1]
    a, b, c = split3(pot[...])
    a, b, c = a.astype(BF16), b.astype(BF16), c.astype(BF16)
    pieces = jnp.concatenate([a, b, c, jnp.zeros_like(a)], 0)
    d = a.shape[0]

    @pl.loop(0, ends.shape[1] // tb)
    def _(t):
        cols = pl.ds(pl.multiple_of(t * tb, tb), tb)
        row = lax.broadcasted_iota(jnp.int32, (panels, tb), 0)
        pick = jnp.where(row == ends[0:1, cols], 1.0, 0.0) - jnp.where(
            row == ends[1:2, cols], 1.0, 0.0
        )
        got = dot(pieces, pick.astype(BF16), 1, 0)
        out[:, cols] = base[:, cols] + (got[:d] + got[d : 2 * d]) + got[2 * d : 3 * d]


def end_difference(ends, pot, base):
    return pl.pallas_call(
        ends_kernel,
        out_shape=jax.ShapeDtypeStruct(base.shape, F32),
        in_specs=[pl.BlockSpec(memory_space=pltpu.VMEM)] * 3,
        out_specs=pl.BlockSpec(memory_space=pltpu.VMEM),
        compiler_params=pltpu.CompilerParams(vmem_limit_bytes=40 * 2**20),
        name="end_difference",
    )(ends, pot, base)


def exchange_kernel(axes, add, src, out, recv, send_sem, recv_sem):
    count = recv.shape[0]
    me = lax.axis_index(axes)
    cols = lax.axis_size("col")
    my_col = lax.axis_index("col")

    def device(k):
        other = lax.rem(me + k, count)
        if len(axes) == 1:
            return other, (other, my_col)
        return other, (other // cols, lax.rem(other, cols))

    def copy(k):
        other, place = device(k)
        return pltpu.make_async_remote_copy(
            src_ref=src.at[other] if add else src,
            dst_ref=recv.at[k],
            send_sem=send_sem.at[k],
            recv_sem=recv_sem.at[k],
            device_id=place,
            device_id_type=pl.DeviceIdType.MESH,
        )

    barrier = pltpu.get_barrier_semaphore()

    def greet(k, carry):
        pl.semaphore_signal(
            barrier, inc=1, device_id=device(k)[1], device_id_type=pl.DeviceIdType.MESH
        )
        return carry

    lax.fori_loop(1, count, greet, 0)
    pl.semaphore_wait(barrier, count - 1)

    def start(k, carry):
        copy(k).start()
        return carry

    lax.fori_loop(1, count, start, 0)
    if add:

        def finish(k, total):
            copy(k).wait()
            return total + recv[k]

        out[...] = lax.fori_loop(1, count, finish, src[me])
    else:
        out[me] = src[...]

        def finish(k, carry):
            copy(k).wait()
            out[lax.rem(me + count - k, count)] = recv[k]
            return carry

        lax.fori_loop(1, count, finish, 0)


def exchange(x, axes, count, add, number):
    block = x.shape[1:] if add else x.shape
    return pl.pallas_call(
        functools.partial(exchange_kernel, axes, add),
        out_shape=jax.ShapeDtypeStruct(block if add else (count, *block), x.dtype),
        in_specs=[pl.BlockSpec(memory_space=pltpu.VMEM)],
        out_specs=pl.BlockSpec(memory_space=pltpu.VMEM),
        scratch_shapes=[
            pltpu.VMEM((count, *block), x.dtype),
            pltpu.SemaphoreType.DMA((count,)),
            pltpu.SemaphoreType.DMA((count,)),
        ],
        compiler_params=pltpu.CompilerParams(
            collective_id=number, has_side_effects=True, vmem_limit_bytes=24 * 2**20
        ),
        name="exchange_sum" if add else "exchange_gather",
    )(x)


def per_device(
    currents, src_pos, src_dir, cell_ends, pan_pos, tgt_pos, tgt_dir, tgt_ends, wpan_pos
):
    doubled = currents.shape[0]
    half = doubled // 2
    col_count = lax.axis_size("col")
    rows = lax.axis_size("row")
    panel_dev = pan_pos.shape[1]
    block_len = panel_dev * rows
    tdev, wdev = tgt_pos.shape[1], wpan_pos.shape[1]
    packed = jnp.concatenate(
        [
            tgt_pos.reshape(-1),
            tgt_dir.reshape(-1),
            wpan_pos.reshape(-1),
            tgt_ends.astype(F32).reshape(-1),
        ]
    ).reshape(-1, 128)
    packed = exchange(packed, ("row",), rows, False, 0).reshape(rows, -1)

    cur16 = currents.astype(BF16)
    cur_wide = lax.reduce_precision(currents, 8, 7)
    local_ends = cell_ends // (panel_dev * col_count) * panel_dev + cell_ends % panel_dev
    partial_value = spread(local_ends, cur_wide, block_len)
    charge = lax.psum_scatter(partial_value, "row", scatter_dimension=1, tiled=True)

    def whole(start, width, dims=3):
        piece = packed[:, start : start + dims * width].reshape(rows, dims, width)
        return piece.transpose(1, 0, 2).reshape(dims, rows * width)

    tpos = whole(0, tdev)
    tdir = whole(3 * tdev, tdev)
    wpos = whole(6 * tdev, wdev)
    tend = whole(6 * tdev + 3 * wdev, tdev, 2).astype(jnp.int32)
    induct = sweep(
        point_features(tpos, True),
        point_features(src_pos, False).T,
        vector_features(tdir, True),
        vector_features(src_dir, False).T,
        cur16,
    )
    field = sweep(
        point_features(wpos, True),
        point_features(pan_pos, False).T,
        None,
        None,
        charge.astype(BF16),
    )
    pscale = 0.25 / math.sqrt(PANELS)
    lscale = 1.0 / math.sqrt(CELLS)
    potential = jnp.concatenate([field[half:], -field[:half]], 0) * pscale
    voltage = jnp.concatenate([-induct[half:], induct[:half]], 0) * lscale
    total = end_difference(tend, potential, voltage)
    count = rows * col_count
    blocks = total.reshape(doubled, count, -1).transpose(1, 0, 2)
    return exchange(blocks, ("row", "col"), count, True, 1)


def solution(mesh):
    return jax.shard_map(
        per_device,
        mesh=mesh,
        in_specs=(
            P(None, ("row", "col")),
            P(None, ("row", "col")),
            P(None, ("row", "col")),
            P(None, ("row", "col")),
            P(None, ("row", "col")),
            P(None, "row"),
            P(None, "row"),
            P(None, "row"),
            P(None, "row"),
        ),
        out_specs=P(None, ("row", "col")),
        check_vma=False,
    )
```

```python
import functools
import math

import jax
import jax.numpy as jnp
from jax import lax
from jax.experimental import pallas as pl
from jax.experimental.pallas import tpu as pltpu
from jax.sharding import PartitionSpec as P

CELLS = 131072
PANELS = 65536

soft_sq = 0.0004
wave_num = 12.0
turn = wave_num / (2 * math.pi)

A1, A0, K1 = -2.24750753, 1.37545559, 2.2830122
B2, B1, B0 = -3.52005613, 4.32182737, -0.87613445
ENTRY = 2 * K1 * K1
MAGIC = 12582912.0

F32 = jnp.float32
BF16 = jnp.bfloat16


def split3(x):
    a = lax.reduce_precision(x, 8, 7)
    b = lax.reduce_precision(x - a, 8, 7)
    c = lax.reduce_precision(x - a - b, 8, 7)
    return a, b, c


def point_features(pos, is_target):
    x = (pos - 0.5) * turn
    sq = jnp.sum(x * x, axis=0, keepdims=True)
    if is_target:
        sq = sq + soft_sq * turn * turn
        x = -2.0 * x
    a, b, c = split3(x)
    n = split3(sq)
    one = jnp.ones((3, pos.shape[1]), F32)
    pad = jnp.zeros((8, pos.shape[1]), F32)
    if is_target:
        rows = [a, a, a, b, b, c, *n, one, pad]
    else:
        rows = [a, b, c, a, b, a, one, *n, pad]
    return jnp.concatenate(rows, 0).astype(BF16)


def vector_features(vec, is_target):
    a, b, c = split3(vec)
    pad = jnp.zeros((14, vec.shape[1]), F32)
    rows = [a, a, a, b, b, c, pad] if is_target else [a, b, c, a, b, a, pad]
    return jnp.concatenate(rows, 0).astype(BF16)


def entries(dist, weight):
    inverse = lax.rsqrt(dist)
    phase = dist * inverse
    f = phase - ((phase + MAGIC) - MAGIC)
    z = f * f
    s = ((z + A1) * z + A0) * f
    c = ((z + B2) * z + B1) * z + B0
    m = inverse if weight is None else inverse * weight
    real_part = (1.0 / ENTRY - s * s) * m
    imag_part = (s * m) * c
    return real_part.astype(BF16), imag_part.astype(BF16)


def dot(a, b, da, db):
    return lax.dot_general(a, b, (((da,), (db,)), ((), ())), preferred_element_type=F32)


def sweep_kernel(tb, sb, unroll, with_dir, *refs):
    if with_dir:
        ft, fs, gt, gs, wr, wi, out = refs
    else:
        ft, fs, wr, wi, out = refs
    targets = ft.shape[1]
    sources = fs.shape[0]

    @pl.loop(0, targets // tb)
    def _(t):
        tcol = pl.ds(pl.multiple_of(t * tb, tb), tb)
        fcol = ft[:, tcol]
        gcol = gt[:, tcol] if with_dir else None

        def step(j, acc):
            for u in range(unroll):
                start = pl.multiple_of((j * unroll + u) * sb, sb)
                rows = pl.ds(start, sb)
                dist = dot(fs[rows, :], fcol, 1, 0)
                weight = dot(gs[rows, :], gcol, 1, 0) if with_dir else None
                re, im = entries(dist, weight)
                acc = acc + dot(wr[:, rows], re, 1, 0) + dot(wi[:, rows], im, 1, 0)
            return acc

        out[:, tcol] = lax.fori_loop(
            0, sources // (sb * unroll), step, jnp.zeros((wr.shape[0], tb), F32)
        )


def sweep(ft, fs, gt, gs, source, tb=1024, sb=256, unroll=2):
    half = source.shape[0] // 2
    targets, sources = ft.shape[1], fs.shape[0]
    tb, sb = min(tb, targets), min(sb, sources)
    unroll = min(unroll, sources // sb)
    wi = jnp.concatenate([-0.5 * source[half:], 0.5 * source[:half]], 0)
    args = (ft, fs, source, wi) if gt is None else (ft, fs, gt, gs, source, wi)
    total = targets * sources
    out = pl.pallas_call(
        functools.partial(sweep_kernel, tb, sb, unroll, gt is not None),
        out_shape=jax.ShapeDtypeStruct((source.shape[0], targets), F32),
        in_specs=[pl.BlockSpec(memory_space=pltpu.VMEM)] * len(args),
        out_specs=pl.BlockSpec(memory_space=pltpu.VMEM),
        compiler_params=pltpu.CompilerParams(vmem_limit_bytes=40 * 2**20),
        cost_estimate=pl.CostEstimate(
            flops=total * 1600, bytes_accessed=4 * 2**20, transcendentals=total
        ),
        name="sweep_cells" if gt is not None else "sweep_panels",
    )(*args)
    return out * (ENTRY * turn)


def spread_kernel(ends, cur, out):
    doubled = cur.shape[0]
    lows = out.shape[1]
    highs = out.shape[0] // doubled
    n = ends.shape[1]
    chunk = min(n, 512)

    def step(j, acc):
        cols = pl.ds(pl.multiple_of(j * chunk, chunk), chunk)
        for e in range(2):
            idx = ends[e : e + 1, cols]
            hi = idx // lows
            lo = idx - hi * lows
            hit = lax.broadcasted_iota(jnp.int32, (highs, chunk), 0) == hi
            low = jnp.where(
                lax.broadcasted_iota(jnp.int32, (lows, chunk), 0) == lo, 1.0 - 2.0 * e, 0.0
            ).astype(BF16)
            rows = [jnp.where(hit, cur[r : r + 1, cols], 0.0) for r in range(doubled)]
            acc = acc + dot(jnp.concatenate(rows, 0).astype(BF16), low, 1, 1)
        return acc

    out[...] = lax.fori_loop(0, n // chunk, step, jnp.zeros(out.shape, F32))


def spread(ends, cur_wide, block_len):
    doubled = cur_wide.shape[0]
    lows = 256
    highs = block_len // lows
    out = pl.pallas_call(
        spread_kernel,
        out_shape=jax.ShapeDtypeStruct((doubled * highs, lows), F32),
        in_specs=[pl.BlockSpec(memory_space=pltpu.VMEM)] * 2,
        out_specs=pl.BlockSpec(memory_space=pltpu.VMEM),
        compiler_params=pltpu.CompilerParams(vmem_limit_bytes=40 * 2**20),
        name="spread_charges",
    )(ends, cur_wide)
    return out.reshape(doubled, block_len)


def ends_kernel(ends, pot, base, out):
    tb = 256
    panels = pot.shape[1]
    a, b, c = split3(pot[...])
    a, b, c = a.astype(BF16), b.astype(BF16), c.astype(BF16)
    pieces = jnp.concatenate([a, b, c, jnp.zeros_like(a)], 0)
    d = a.shape[0]

    @pl.loop(0, ends.shape[1] // tb)
    def _(t):
        cols = pl.ds(pl.multiple_of(t * tb, tb), tb)
        row = lax.broadcasted_iota(jnp.int32, (panels, tb), 0)
        pick = jnp.where(
            row == ends[0:1, cols], 1.0, jnp.where(row == ends[1:2, cols], -1.0, 0.0)
        )
        got = dot(pieces, pick.astype(BF16), 1, 0)
        out[:, cols] = base[:, cols] + (got[:d] + got[d : 2 * d]) + got[2 * d : 3 * d]


def end_difference(ends, pot, base):
    return pl.pallas_call(
        ends_kernel,
        out_shape=jax.ShapeDtypeStruct(base.shape, F32),
        in_specs=[pl.BlockSpec(memory_space=pltpu.VMEM)] * 3,
        out_specs=pl.BlockSpec(memory_space=pltpu.VMEM),
        compiler_params=pltpu.CompilerParams(vmem_limit_bytes=40 * 2**20),
        name="end_difference",
    )(ends, pot, base)


def exchange_kernel(axes, add, src, out, recv, send_sem, recv_sem):
    count = recv.shape[0]
    me = lax.axis_index(axes)
    cols = lax.axis_size("col")
    my_col = lax.axis_index("col")

    def device(k):
        other = lax.rem(me + k, count)
        if len(axes) == 1:
            return other, (other, my_col)
        return other, (other // cols, lax.rem(other, cols))

    def copy(k):
        other, place = device(k)
        return pltpu.make_async_remote_copy(
            src_ref=src.at[other] if add else src,
            dst_ref=recv.at[k],
            send_sem=send_sem.at[k],
            recv_sem=recv_sem.at[k],
            device_id=place,
            device_id_type=pl.DeviceIdType.MESH,
        )

    barrier = pltpu.get_barrier_semaphore()

    def greet(k, carry):
        pl.semaphore_signal(
            barrier, inc=1, device_id=device(k)[1], device_id_type=pl.DeviceIdType.MESH
        )
        return carry

    lax.fori_loop(1, count, greet, 0)
    pl.semaphore_wait(barrier, count - 1)

    def start(k, carry):
        copy(k).start()
        return carry

    lax.fori_loop(1, count, start, 0)
    if add:

        def finish(k, total):
            copy(k).wait()
            return total + recv[k]

        out[...] = lax.fori_loop(1, count, finish, src[me])
    else:
        out[me] = src[...]

        def finish(k, carry):
            copy(k).wait()
            out[lax.rem(me + count - k, count)] = recv[k]
            return carry

        lax.fori_loop(1, count, finish, 0)


def exchange(x, axes, count, add, number):
    block = x.shape[1:] if add else x.shape
    return pl.pallas_call(
        functools.partial(exchange_kernel, axes, add),
        out_shape=jax.ShapeDtypeStruct(block if add else (count, *block), x.dtype),
        in_specs=[pl.BlockSpec(memory_space=pltpu.VMEM)],
        out_specs=pl.BlockSpec(memory_space=pltpu.VMEM),
        scratch_shapes=[
            pltpu.VMEM((count, *block), x.dtype),
            pltpu.SemaphoreType.DMA((count,)),
            pltpu.SemaphoreType.DMA((count,)),
        ],
        compiler_params=pltpu.CompilerParams(
            collective_id=number, has_side_effects=True, vmem_limit_bytes=24 * 2**20
        ),
        name="exchange_sum" if add else "exchange_gather",
    )(x)


def per_device(
    currents, src_pos, src_dir, cell_ends, pan_pos, tgt_pos, tgt_dir, tgt_ends, wpan_pos
):
    doubled = currents.shape[0]
    half = doubled // 2
    col_count = lax.axis_size("col")
    rows = lax.axis_size("row")
    panel_dev = pan_pos.shape[1]
    block_len = panel_dev * rows
    tdev, wdev = tgt_pos.shape[1], wpan_pos.shape[1]
    packed = jnp.concatenate(
        [
            tgt_pos.reshape(-1),
            tgt_dir.reshape(-1),
            wpan_pos.reshape(-1),
            tgt_ends.astype(F32).reshape(-1),
        ]
    ).reshape(-1, 128)
    packed = exchange(packed, ("row",), rows, False, 0).reshape(rows, -1)

    cur16 = currents.astype(BF16)
    cur_wide = lax.reduce_precision(currents, 8, 7)
    local_ends = cell_ends // (panel_dev * col_count) * panel_dev + cell_ends % panel_dev
    partial_value = spread(local_ends, cur_wide, block_len)
    charge = lax.psum_scatter(partial_value, "row", scatter_dimension=1, tiled=True)

    def whole(start, width, dims=3):
        piece = packed[:, start : start + dims * width].reshape(rows, dims, width)
        return piece.transpose(1, 0, 2).reshape(dims, rows * width)

    tpos = whole(0, tdev)
    tdir = whole(3 * tdev, tdev)
    wpos = whole(6 * tdev, wdev)
    tend = whole(6 * tdev + 3 * wdev, tdev, 2).astype(jnp.int32)
    induct = sweep(
        point_features(tpos, True),
        point_features(src_pos, False).T,
        vector_features(tdir, True),
        vector_features(src_dir, False).T,
        cur16,
    )
    field = sweep(
        point_features(wpos, True),
        point_features(pan_pos, False).T,
        None,
        None,
        charge.astype(BF16),
    )
    pscale = 0.25 / math.sqrt(PANELS)
    lscale = 1.0 / math.sqrt(CELLS)
    potential = jnp.concatenate([field[half:], -field[:half]], 0) * pscale
    voltage = jnp.concatenate([-induct[half:], induct[:half]], 0) * lscale
    total = end_difference(tend, potential, voltage)
    count = rows * col_count
    blocks = total.reshape(doubled, count, -1).transpose(1, 0, 2)
    return exchange(blocks, ("row", "col"), count, True, 1)


def solution(mesh):
    return jax.shard_map(
        per_device,
        mesh=mesh,
        in_specs=(
            P(None, ("row", "col")),
            P(None, ("row", "col")),
            P(None, ("row", "col")),
            P(None, ("row", "col")),
            P(None, ("row", "col")),
            P(None, "row"),
            P(None, "row"),
            P(None, "row"),
            P(None, "row"),
        ),
        out_specs=P(None, ("row", "col")),
        check_vma=False,
    )
```
